128 devices in a mesh: row: 16 (over x, z), col: 4 (over y_lo, core), grp: 2 (over y_hi).
Axes of the slice: x: 4, y: 4 (y_hi: 2, y_lo: 2; y = y_hi * 2 + y_lo), z: 4, core: 2. Of those that a mesh axis runs over, the one named last changes fastest.
Arguments:
- matrix: float32 [16384, 16384], P('row', ('col', 'grp')), may hold values from -8 to 8, as said below
- basis_rows: float32 [4096, 16384], P(('col', 'grp'), 'row'), may hold values from -6 to 6
- reflectors: float32 [16384, 512], P('row'), may hold values from -0.125 to 0.125
- tfactor: float32 [512, 512], replicated, may hold values from -0.25 to 2, as said below
Outputs:
- new_matrix: float32 [16384, 16384], P('row', ('col', 'grp'))
- new_basis: float32 [4096, 16384], P(('col', 'grp'), 'row')
The draws below stay inside these ranges and needn't reach their ends.
Inputs may be any that keep to these rules, and one draw needn't show every extreme that they name: The matrix A that it represents is symmetric. `tfactor`: upper triangular: zero below the diagonal, diagonal between 1 and 2.
All inputs are finite; a program needn't handle non-finite values.
Results may differ from the reference program's by a relative error of at most 0.000073.
Values sent between devices are 32-bit elements; how exact they have to be, the bound alone decides.
No kernel may reach another device: no remote copies, remote signals or barrier semaphores. Data moves between devices by JAX's collectives and lax.ppermute only.
A program may use at most 128 MiB of HBM per device.

```python
import jax
import jax.numpy as jnp
from jax import lax

M = 16384
NB = 512
ROWBLK = 1024
COLBLK = 2048
SLICE = 128
QROWS = 4096


def draw_matrix(key, part):
    first_key = jax.random.fold_in(key, 11)
    normal = jax.random.normal(first_key, (M, M), jnp.float32)
    symmetric = (normal + normal.T) * 0.70710678
    symmetric = jnp.clip(symmetric, -8.0, 8.0)
    nrow = M // ROWBLK
    ncol = M // COLBLK
    return symmetric.reshape(M, nrow, ncol, SLICE).transpose(0, 2, 1, 3).reshape(M, M)


def draw_tfactor(key, part):
    first_key = jax.random.fold_in(key, 21)
    second_key = jax.random.fold_in(key, 22)
    above = jnp.clip(jax.random.normal(first_key, (NB, NB), jnp.float32) * NB ** (-0.5), -0.25, 0.25)
    diag = jax.random.uniform(second_key, (NB,), jnp.float32, 1.0, 2.0)
    return jnp.triu(above, 1) + jnp.diag(diag)


def shard_levels(own_key, extent, shards, least, top_value):
    level, own = 1.0, jax.random.fold_in(own_key, 6)
    for dim, shards_of in shards:
        heights = jnp.exp(jax.random.uniform(jax.random.fold_in(own, dim), (shards_of,), jnp.float32, least / len(shards), top_value / len(shards)))
        level = level * jnp.repeat(heights, extent[dim] // shards_of).reshape([-1 if axis == dim else 1 for axis in range(len(extent))])
    return level


def gaussian(own_key, dims, deviation, most, pieces=(), held_as=jnp.bfloat16):
    loudness = shard_levels(own_key, dims, pieces, -0.22, 0.18) if pieces else 1.0
    array = jax.random.normal(own_key, dims, jnp.float32) * deviation * loudness
    return jnp.minimum(jnp.maximum(array, -most), most).astype(held_as)


def setup_inputs(seed: int = 0) -> dict:
    splits = jax.random.split(jax.random.key(seed), 5)
    return {
        "matrix": draw_matrix(jax.random.fold_in(splits[4], 71), 0),
        "basis_rows": gaussian(splits[1], (QROWS, M), 1.0, 6.0, ((0, 8), (1, 16)), jnp.float32),
        "reflectors": gaussian(splits[2], (M, NB), (4 * NB) ** -0.5, 0.125, ((0, 16),), jnp.float32),
        "tfactor": draw_tfactor(jax.random.fold_in(splits[4], 71), 0),
    }


def to_global(stored):
    nrow = M // ROWBLK
    ncol = M // COLBLK
    return stored.reshape(M, ncol, nrow, SLICE).transpose(0, 2, 1, 3).reshape(M, M)


def to_stored(full):
    nrow = M // ROWBLK
    ncol = M // COLBLK
    return full.reshape(M, nrow, ncol, SLICE).transpose(0, 2, 1, 3).reshape(M, M)


def reference(matrix, basis_rows, reflectors, tfactor):
    highest = lax.Precision.HIGHEST
    full = to_global(matrix)
    applied = jnp.dot(full, reflectors, precision=highest, preferred_element_type=jnp.float32)
    wide = jnp.dot(applied, tfactor, precision=highest, preferred_element_type=jnp.float32)
    cross = jnp.dot(reflectors.T, wide, precision=highest, preferred_element_type=jnp.float32)
    inner = jnp.dot(tfactor.T, cross, precision=highest, preferred_element_type=jnp.float32)
    zeta = wide - 0.5 * jnp.dot(reflectors, inner, precision=highest, preferred_element_type=jnp.float32)
    updated = full - jnp.dot(reflectors, zeta.T, precision=highest, preferred_element_type=jnp.float32)
    updated = updated - jnp.dot(zeta, reflectors.T, precision=highest, preferred_element_type=jnp.float32)
    q_proj = jnp.dot(basis_rows, reflectors, precision=highest, preferred_element_type=jnp.float32)
    q_fact = jnp.dot(q_proj, tfactor, precision=highest, preferred_element_type=jnp.float32)
    new_basis = basis_rows - jnp.dot(q_fact, reflectors.T, precision=highest, preferred_element_type=jnp.float32)
    return to_stored(updated), new_basis
```

```python
import functools

import jax
import jax.numpy as jnp
import numpy as np
from jax import lax
from jax.experimental import pallas as pl
from jax.experimental.pallas import tpu as pltpu
from jax.sharding import PartitionSpec as P

F32, BF16 = jnp.float32, jnp.bfloat16
EVERY = ("row", "col", "grp")
NN = (((1,), (0,)), ((), ()))
NT = (((1,), (1,)), ((), ()))
TN = (((0,), (0,)), ((), ()))


def flip_ring(i, bit):
    g = (i ^ (i >> 1)) ^ (1 << bit)
    return g ^ (g >> 1)


def linear(x, z, y, core):
    return (x * 4 + z) * 8 + ((y % 2) * 2 + core) * 2 + y // 2


def coords(dev):
    row, member = divmod(dev, 8)
    return row // 4, row % 4, (member % 2) * 2 + member // 4, (member // 2) % 2


def flip(dev, dim):
    x, z, y, core = coords(dev)
    if dim == "c":
        return linear(x, z, y, 1 - core)
    bit = int(dim[1])
    if dim[0] == "x":
        x = flip_ring(x, bit)
    elif dim[0] == "z":
        z = flip_ring(z, bit)
    else:
        y = flip_ring(y, bit)
    return linear(x, z, y, core)


ROW_DIMS = ("x0", "z0", "x1", "z1")


def row_dim(core, half, step):
    return ROW_DIMS[(step + core * 2 + half) % 4]


def y_dim(core, step):
    return "y%d" % ((step + core) % 2)


def relative(dev, dims, j):
    for k, dim in enumerate(dims):
        if j >> k & 1:
            dev = flip(dev, dim)
    return dev


def build_tables():
    out = np.zeros((128, 64), np.int32)
    for dev in range(128):
        core = coords(dev)[3]
        for h in range(2):
            dims = [row_dim(core, h, s) for s in range(4)]
            for j in range(16):
                out[dev, h * 16 + j] = relative(dev, dims, j) // 8
        other = flip(dev, "c")
        for first, base in ((other, 32), (dev, 36)):
            dims = [y_dim(coords(first)[3], s) for s in range(2)]
            for j in range(4):
                out[dev, base + j] = relative(first, dims, j) % 8
        out[dev, 40] = dev % 8
    return out


TABLES = build_tables()


def moved(x, dim_of_core):
    pairs = [(dev, flip(dev, dim_of_core(coords(dev)[3]))) for dev in range(128)]
    return lax.ppermute(x, EVERY, pairs)


def split(x):
    hi = x.astype(BF16)
    return hi, (x - hi.astype(F32)).astype(BF16)


def dot3(a, b, dims):
    def one(u, v):
        return lax.dot_general(u, v, dims, preferred_element_type=F32)

    return one(a[0], b[0]) + (one(a[0], b[1]) + one(a[1], b[0]))


def cost(macs, moved_bytes):
    return pl.CostEstimate(flops=6 * macs, bytes_accessed=moved_bytes, transcendentals=0)


def params(mib):
    return pltpu.CompilerParams(vmem_limit_bytes=mib * 2**20)


def full(shape):
    return pl.BlockSpec(shape, lambda *_: (0,) * len(shape))


def basis_kernel(tab, b_ref, v_ref, q0_ref, q1_ref, q):
    q[...] = dot3(split(b_ref[...]), split(v_ref[...]), NN)
    for h, out in enumerate((q0_ref, q1_ref)):
        for j in range(16):
            place = int("{:04b}".format(j)[::-1], 2)
            rows = pl.ds(pl.multiple_of(tab[h * 16 + j] * 32, 32), 32)
            out[place * 32 : place * 32 + 32, :] = q[rows, h * 256 : h * 256 + 256]


def basis_product(tab, basis, v):
    return pl.pallas_call(
        basis_kernel,
        grid_spec=pltpu.PrefetchScalarGridSpec(
            num_scalar_prefetch=1,
            grid=(1,),
            in_specs=[full((512, 1024)), full((1024, 512))],
            out_specs=[full((512, 256))] * 2,
            scratch_shapes=[pltpu.VMEM((512, 512), F32)],
        ),
        out_shape=[jax.ShapeDtypeStruct((512, 256), F32)] * 2,
        compiler_params=params(32),
        cost_estimate=cost(512 * 1024 * 512, 5 << 20),
    )(tab, basis, v)


def place_blocks(tab, pieces, hi, lo, rows=128):
    for h in range(2):
        for j in range(16):
            src = pieces[h * 2 + j // 8]
            block = src[(j % 8) * rows : (j % 8) * rows + rows, :]
            bh, bl = split(block)
            at = pl.ds(pl.multiple_of(tab[h * 16 + j] * rows, rows), rows)
            hi[at, h * 256 : h * 256 + 256] = bh
            lo[at, h * 256 : h * 256 + 256] = bl


def apply_kernel(tab, a0, a1, a2, a3, p0, p1, p2, p3, send_ref, keep_ref, vh, vl):
    step = pl.program_id(0)

    @pl.when(step == 0)
    def _():
        place_blocks(tab, (p0, p1, p2, p3), vh, vl)

    def product(out):
        for i, a in enumerate((a0, a1, a2, a3)):
            out[i * 128 : i * 128 + 128, :] = dot3(
                split(a[...]), (vh[...], vl[...]), NN
            )

    @pl.when(step == 0)
    def _():
        product(send_ref)

    @pl.when(step == 1)
    def _():
        product(keep_ref)


def apply_matrix(tab, matrix, pieces):
    def a_spec(i):
        return pl.BlockSpec((128, 2048), lambda s, t, i=i: (t[32 + s * 4 + i], 0))

    return pl.pallas_call(
        apply_kernel,
        grid_spec=pltpu.PrefetchScalarGridSpec(
            num_scalar_prefetch=1,
            grid=(2,),
            in_specs=[a_spec(i) for i in range(4)] + [full((1024, 256))] * 4,
            out_specs=[full((512, 512))] * 2,
            scratch_shapes=[pltpu.VMEM((2048, 512), BF16)] * 2,
        ),
        out_shape=[jax.ShapeDtypeStruct((512, 512), F32)] * 2,
        compiler_params=params(40),
        cost_estimate=cost(1024 * 2048 * 512, 14 << 20),
    )(tab, matrix, matrix, matrix, matrix, *pieces)


def inner_kernel(tab, v_ref, s_ref, k_ref, gs_ref, gk_ref, g):
    total = None
    for base, src in ((32, s_ref), (36, k_ref)):
        rows = [
            v_ref[pl.ds(pl.multiple_of(tab[base + i] * 128, 128), 128), :]
            for i in range(4)
        ]
        v = jnp.concatenate(rows, axis=0)
        part = dot3(split(v), split(src[...]), TN)
        total = part if total is None else total + part
    g[...] = total
    for base, out in ((32, gs_ref), (36, gk_ref)):
        for i in range(4):
            at = pl.ds(pl.multiple_of(tab[base + i] * 64, 64), 64)
            out[i * 64 : i * 64 + 64, :] = g[at, :]


def inner_product(tab, v, send, keep):
    return pl.pallas_call(
        inner_kernel,
        grid_spec=pltpu.PrefetchScalarGridSpec(
            num_scalar_prefetch=1,
            grid=(1,),
            in_specs=[full((1024, 512)), full((512, 512)), full((512, 512))],
            out_specs=[full((256, 512))] * 2,
            scratch_shapes=[pltpu.VMEM((512, 512), F32)],
        ),
        out_shape=[jax.ShapeDtypeStruct((256, 512), F32)] * 2,
        compiler_params=params(32),
        cost_estimate=cost(1024 * 512 * 512, 5 << 20),
    )(tab, v, send, keep)


def turned_kernel(tab, t_ref, v_ref, p0, p1, p2, p3, ch, cl, rh, rl, vh, vl):
    t = split(t_ref[...])
    place_blocks(tab, (p0, p1, p2, p3), vh, vl)
    for i in range(4):
        at = slice(i * 512, i * 512 + 512)
        ch[at, :], cl[at, :] = split(dot3((vh[at, :], vl[at, :]), t, NT))
    for i in range(2):
        at = slice(i * 512, i * 512 + 512)
        rh[at, :], rl[at, :] = split(dot3(split(v_ref[at, :]), t, NT))


def turned(tab, tfactor, v, pieces):
    return pl.pallas_call(
        turned_kernel,
        grid_spec=pltpu.PrefetchScalarGridSpec(
            num_scalar_prefetch=1,
            grid=(1,),
            in_specs=[full((512, 512)), full((1024, 512))] + [full((1024, 256))] * 4,
            out_specs=[full((2048, 512))] * 2 + [full((1024, 512))] * 2,
            scratch_shapes=[pltpu.VMEM((2048, 512), BF16)] * 2,
        ),
        out_shape=[jax.ShapeDtypeStruct((2048, 512), BF16)] * 2
        + [jax.ShapeDtypeStruct((1024, 512), BF16)] * 2,
        compiler_params=params(48),
        cost_estimate=cost(3072 * 512 * 512, 13 << 20),
    )(tab, tfactor, v, *pieces)


def rows_kernel(tab, wk_ref, ws_ref, gk_ref, gs_ref, rh, rl, oh, ol, g, w):
    for base, gsrc, wsrc in ((36, gk_ref, wk_ref), (32, gs_ref, ws_ref)):
        for i in range(4):
            g[pl.ds(pl.multiple_of(tab[base + i] * 64, 64), 64), :] = gsrc[
                i * 64 : i * 64 + 64, :
            ]
            w[pl.ds(pl.multiple_of(tab[base + i] * 128, 128), 128), :] = wsrc[
                i * 128 : i * 128 + 128, :
            ]
    gg = split(g[...])
    for i in range(2):
        at = slice(i * 512, i * 512 + 512)
        oh[at, :], ol[at, :] = split(w[at, :] - dot3((rh[at, :], rl[at, :]), gg, NN))


def rows_less(tab, w_keep, w_other, g_keep, g_other, rh, rl):
    return pl.pallas_call(
        rows_kernel,
        grid_spec=pltpu.PrefetchScalarGridSpec(
            num_scalar_prefetch=1,
            grid=(1,),
            in_specs=[full((512, 512))] * 2
            + [full((256, 512))] * 2
            + [full((1024, 512))] * 2,
            out_specs=[full((1024, 512))] * 2,
            scratch_shapes=[pltpu.VMEM((512, 512), F32), pltpu.VMEM((1024, 512), F32)],
        ),
        out_shape=[jax.ShapeDtypeStruct((1024, 512), BF16)] * 2,
        compiler_params=params(40),
        cost_estimate=cost(1024 * 512 * 512, 7 << 20),
    )(tab, w_keep, w_other, g_keep, g_other, rh, rl)


def update_kernel(tab, a, p0, p1, p2, p3, ch, cl, rh, rl, oh, ol, out, wh, wl, lh, ll):
    step = pl.program_id(0)

    @pl.when(step == 0)
    def _():
        place_blocks(tab, (p0, p1, p2, p3), wh, wl)
        lh[:, :512] = rh[...]
        ll[:, :512] = rl[...]
        lh[:, 512:] = oh[...]
        ll[:, 512:] = ol[...]

    at = pl.ds(pl.multiple_of(step * 256, 256), 256)
    right_h = jnp.concatenate([wh[at, :], ch[at, :]], axis=1)
    right_l = jnp.concatenate([wl[at, :], cl[at, :]], axis=1)
    for i in range(4):
        rows = slice(i * 256, i * 256 + 256)
        out[rows, :] = a[rows, :] - dot3(
            (lh[rows, :], ll[rows, :]), (right_h, right_l), NT
        )


def update(tab, matrix, pieces, ch, cl, rh, rl, oh, ol):
    return pl.pallas_call(
        update_kernel,
        grid_spec=pltpu.PrefetchScalarGridSpec(
            num_scalar_prefetch=1,
            grid=(8,),
            in_specs=[pl.BlockSpec((1024, 256), lambda s, t: (0, s))]
            + [full((1024, 256))] * 4
            + [full((2048, 512))] * 2
            + [full((1024, 512))] * 4,
            out_specs=pl.BlockSpec((1024, 256), lambda s, t: (0, s)),
            scratch_shapes=[pltpu.VMEM((2048, 512), BF16)] * 2
            + [pltpu.VMEM((1024, 1024), BF16)] * 2,
        ),
        out_shape=jax.ShapeDtypeStruct((1024, 2048), F32),
        compiler_params=params(50),
        cost_estimate=cost(2 * 1024 * 2048 * 512, 28 << 20),
    )(tab, matrix, *pieces, ch, cl, rh, rl, oh, ol)


def basis_update_kernel(tab, b_ref, p0, p1, p2, p3, rh, rl, out, qh, ql):
    place_blocks(tab, (p0, p1, p2, p3), qh, ql, 32)
    out[...] = b_ref[...] - dot3((qh[...], ql[...]), (rh[...], rl[...]), NT)


def basis_update(tab, basis, pieces, rh, rl):
    return pl.pallas_call(
        basis_update_kernel,
        grid_spec=pltpu.PrefetchScalarGridSpec(
            num_scalar_prefetch=1,
            grid=(1,),
            in_specs=[full((512, 1024))]
            + [full((256, 256))] * 4
            + [full((1024, 512))] * 2,
            out_specs=full((512, 1024)),
            scratch_shapes=[pltpu.VMEM((512, 512), BF16)] * 2,
        ),
        out_shape=jax.ShapeDtypeStruct((512, 1024), F32),
        compiler_params=params(32),
        cost_estimate=cost(512 * 1024 * 512, 7 << 20),
    )(tab, basis, *pieces, rh, rl)


def on_device(matrix, basis_rows, reflectors, tfactor):
    dev = lax.axis_index(EVERY)
    tab = lax.dynamic_index_in_dim(jnp.asarray(TABLES), dev, 0, keepdims=False)
    own_v = lax.dynamic_slice_in_dim(reflectors, tab[40] * 128, 128, 0)

    q = list(basis_product(tab, basis_rows, reflectors))
    v = [own_v[:, :256], own_v[:, 256:]]
    last_v = [None, None]
    for s in range(4):
        for h in range(2):
            half = q[h].shape[0] // 2
            message = jnp.concatenate([v[h], q[h][half:]], axis=0)
            got = moved(message, lambda c: row_dim(c, h, s))
            n = v[h].shape[0]
            q[h] = q[h][:half] + got[n:]
            if s < 3:
                v[h] = jnp.concatenate([v[h], got[:n]], axis=0)
            else:
                last_v[h] = got[:n]
    v_pieces = (v[0], last_v[0], v[1], last_v[1])

    send, keep = apply_matrix(tab, matrix, v_pieces)
    w = keep + moved(send, lambda c: "c")
    g_send, g_keep = inner_product(tab, reflectors, send, keep)
    g = g_keep + moved(g_send, lambda c: "c")
    w, g = w.reshape(4, 128, 512), g.reshape(4, 64, 512)
    for s in range(2):
        w = w.reshape(-1, 2, 128, 512)
        g = g.reshape(-1, 2, 64, 512)
        n = w.shape[0]
        message = jnp.concatenate(
            [w[:, 1].reshape(n * 128, 512), g[:, 1].reshape(n * 64, 512)], axis=0
        )
        got = moved(message, lambda c: y_dim(c, s))
        w = w[:, 0] + got[: n * 128].reshape(n, 128, 512)
        g = g[:, 0] + got[n * 128 :].reshape(n, 64, 512)
    w, g = w.reshape(128, 512), g.reshape(64, 512)

    ch, cl, rh, rl = turned(tab, tfactor, reflectors, v_pieces)

    wc = [w[:, :256], w[:, 256:]]
    last_w, last_q = [None, None], [None, None]
    w_rows = w
    for s in range(4):
        g = g + moved(g, lambda c: row_dim(c, 0, s))
        for h in range(2):
            n = wc[h].shape[0]
            got = moved(
                jnp.concatenate([wc[h], q[h]], axis=0), lambda c: row_dim(c, h, s)
            )
            if s < 3:
                wc[h] = jnp.concatenate([wc[h], got[:n]], axis=0)
                q[h] = jnp.concatenate([q[h], got[n:]], axis=0)
            else:
                last_w[h], last_q[h] = got[:n], got[n:]
        if s < 2:
            w_rows = jnp.concatenate(
                [w_rows, moved(w_rows, lambda c: y_dim(c, s))], axis=0
            )
    w_other = moved(w_rows, lambda c: "c")
    for s in range(2):
        g = jnp.concatenate([g, moved(g, lambda c: y_dim(c, s))], axis=0)
    g_other = moved(g, lambda c: "c")

    new_basis = basis_update(tab, basis_rows, (q[0], last_q[0], q[1], last_q[1]), rh, rl)
    oh, ol = rows_less(tab, w_rows, w_other, g, g_other, rh, rl)
    new_matrix = update(
        tab, matrix, (wc[0], last_w[0], wc[1], last_w[1]), ch, cl, rh, rl, oh, ol
    )
    return new_matrix, new_basis


def solution(mesh):
    placed = (P("row", ("col", "grp")), P(("col", "grp"), "row"), P("row", None), P())
    return jax.shard_map(
        on_device,
        mesh=mesh,
        in_specs=placed,
        out_specs=(P("row", ("col", "grp")), P(("col", "grp"), "row")),
        check_vma=False,
    )
```

```python
import jax
import jax.numpy as jnp
import numpy as np
from jax import lax
from jax.experimental import pallas as pl
from jax.experimental.pallas import tpu as pltpu
from jax.sharding import PartitionSpec as P

F32, BF16 = jnp.float32, jnp.bfloat16
EVERY = ("row", "col", "grp")
NN = (((1,), (0,)), ((), ()))
NT = (((1,), (1,)), ((), ()))
TN = (((0,), (0,)), ((), ()))


def flip_ring(i, bit):
    g = (i ^ (i >> 1)) ^ (1 << bit)
    return g ^ (g >> 1)


def linear(x, z, y, core):
    return (x * 4 + z) * 8 + ((y % 2) * 2 + core) * 2 + y // 2


def coords(dev):
    row, member = divmod(dev, 8)
    return row // 4, row % 4, (member % 2) * 2 + member // 4, (member // 2) % 2


def flip(dev, dim):
    x, z, y, core = coords(dev)
    if dim == "c":
        return linear(x, z, y, 1 - core)
    bit = int(dim[1])
    if dim[0] == "x":
        x = flip_ring(x, bit)
    elif dim[0] == "z":
        z = flip_ring(z, bit)
    else:
        y = flip_ring(y, bit)
    return linear(x, z, y, core)


ROW_DIMS = {
    (0, 0): ("x0", "z0", "x1", "z1"),
    (1, 0): ("z0", "x0", "z1", "x1"),
    (0, 1): ("x1", "z1", "x0", "z0"),
    (1, 1): ("z1", "x1", "z0", "x0"),
}


def row_dim(core, half, step):
    return ROW_DIMS[core, half][step]


def y_dim(core, step):
    return "y%d" % ((step + core) % 2)


def relative(dev, dims, j):
    for k, dim in enumerate(dims):
        if j >> k & 1:
            dev = flip(dev, dim)
    return dev


def build_tables():
    out = np.zeros((128, 64), np.int32)
    for dev in range(128):
        core = coords(dev)[3]
        for h in range(2):
            dims = [row_dim(core, h, s) for s in range(4)]
            for j in range(16):
                out[dev, h * 16 + j] = relative(dev, dims, j) // 8
        other = flip(dev, "c")
        for first, base in ((other, 32), (dev, 36)):
            dims = [y_dim(coords(first)[3], s) for s in range(2)]
            for j in range(4):
                out[dev, base + j] = relative(first, dims, j) % 8
        out[dev, 40] = dev % 8
    return out


TABLES = build_tables()


def moved(x, dim_of_core):
    pairs = [(dev, flip(dev, dim_of_core(coords(dev)[3]))) for dev in range(128)]
    return lax.ppermute(x, EVERY, pairs)


def split(x):
    hi = x.astype(BF16)
    return hi, (x - hi.astype(F32)).astype(BF16)


def dot3(a, b, dims):
    def one(u, v):
        return lax.dot_general(u, v, dims, preferred_element_type=F32)

    return one(a[0], b[0]) + (one(a[0], b[1]) + one(a[1], b[0]))


def cost(macs, moved_bytes):
    return pl.CostEstimate(flops=6 * macs, bytes_accessed=moved_bytes, transcendentals=0)


def params(mib):
    return pltpu.CompilerParams(vmem_limit_bytes=mib * 2**20)


def in_hbm(x):
    return pltpu.with_memory_space_constraint(x, pltpu.HBM)


def in_vmem(x):
    return pltpu.with_memory_space_constraint(x, pltpu.VMEM)


WHOLE = pl.BlockSpec(memory_space=pltpu.VMEM)


def full(shape):
    return pl.BlockSpec(shape, lambda *_: (0,) * len(shape))


def tiled(shape):
    return pl.BlockSpec(shape, lambda s, t: (s, 0))


def basis_kernel(tab, b_ref, v_ref, q0_ref, q1_ref, q, vh, vl):
    step = pl.program_id(0)

    @pl.when(step == 0)
    def _():
        vh[...], vl[...] = split(v_ref[...])

    rows = pl.ds(pl.multiple_of(step * 128, 128), 128)
    q[rows, :] = dot3(split(b_ref[...]), (vh[...], vl[...]), NN)

    @pl.when(step == 3)
    def _():
        for h, out in enumerate((q0_ref, q1_ref)):
            for j in range(16):
                place = (j >> 1 & 1) * 8 + (j >> 2 & 1) * 4 + (j >> 3 & 1) * 2 + (j & 1)
                rows = pl.ds(pl.multiple_of(tab[h * 16 + j] * 32, 32), 32)
                out[place * 32 : place * 32 + 32, :] = q[rows, h * 256 : h * 256 + 256]


def basis_product(tab, basis, v):
    return pl.pallas_call(
        basis_kernel,
        grid_spec=pltpu.PrefetchScalarGridSpec(
            num_scalar_prefetch=1,
            grid=(4,),
            in_specs=[tiled((128, 1024)), full((1024, 512))],
            out_specs=[full((512, 256))] * 2,
            scratch_shapes=[pltpu.VMEM((512, 512), F32)]
            + [pltpu.VMEM((1024, 512), BF16)] * 2,
        ),
        out_shape=[jax.ShapeDtypeStruct((512, 256), F32)] * 2,
        compiler_params=params(16),
        cost_estimate=cost(512 * 1024 * 512, 5 << 20),
    )(tab, in_hbm(basis), in_hbm(v))


def place_blocks(tab, pieces, hi, lo, rows=128):
    for h in range(2):
        for j in range(16):
            src = pieces[h * 2 + j // 8]
            block = src[(j % 8) * rows : (j % 8) * rows + rows, :]
            bh, bl = split(block)
            at = pl.ds(pl.multiple_of(tab[h * 16 + j] * rows, rows), rows)
            hi[at, h * 256 : h * 256 + 256] = bh
            lo[at, h * 256 : h * 256 + 256] = bl


def apply_part(tab, first, a_refs, pieces, ah, al, vh, vl, out, add):
    @pl.when(pl.program_id(0) == 0)
    def _():
        for h in range(2):
            vh[h], vl[h] = split(pieces[h][...])

    for h in range(2):
        for i, a in enumerate(a_refs):
            for j in range(8):
                at = tab[h * 16 + first + j] * 128
                block = a[:, pl.ds(pl.multiple_of(at, 128), 128)]
                rows, lanes = slice(i * 128, i * 128 + 128), slice(j * 128, j * 128 + 128)
                ah[rows, lanes], al[rows, lanes] = split(block)
        part = dot3((ah[...], al[...]), (vh[h], vl[h]), NN)
        lanes = slice(h * 256, h * 256 + 256)
        out[:, lanes] = part if add is None else part + add[:, lanes]


def apply_first_kernel(tab, a0, a1, a2, a3, p0, p1, out, ah, al, vh, vl):
    apply_part(tab, 0, (a0, a1, a2, a3), (p0, p1), ah, al, vh, vl, out, None)


def apply_last_kernel(tab, a0, a1, a2, a3, p0, p1, acc, send, keep, ah, al, vh, vl):
    for s, out in enumerate((send, keep)):

        @pl.when(pl.program_id(0) == s)
        def _(out=out):
            apply_part(tab, 8, (a0, a1, a2, a3), (p0, p1), ah, al, vh, vl, out, acc)


def apply_matrix(tab, matrix, pieces, acc=None):
    def a_spec(i):
        return pl.BlockSpec((128, 2048), lambda s, t, i=i: (t[32 + s * 4 + i], 0))

    tile = pl.BlockSpec((512, 512), lambda s, t: (s, 0))
    last = acc is not None
    return pl.pallas_call(
        apply_last_kernel if last else apply_first_kernel,
        grid_spec=pltpu.PrefetchScalarGridSpec(
            num_scalar_prefetch=1,
            grid=(2,),
            in_specs=[a_spec(i) for i in range(4)]
            + [full((1024, 256))] * 2
            + [tile] * last,
            out_specs=[full((512, 512))] * 2 if last else tile,
            scratch_shapes=[pltpu.VMEM((512, 1024), BF16)] * 2
            + [pltpu.VMEM((2, 1024, 256), BF16)] * 2,
        ),
        out_shape=[jax.ShapeDtypeStruct((512, 512), F32)] * 2
        if last
        else jax.ShapeDtypeStruct((1024, 512), F32),
        compiler_params=params(28),
        cost_estimate=cost(1024 * 1024 * 512, 12 << 20),
    )(tab, *[matrix] * 4, *pieces, *([acc] if last else []))


def inner_kernel(tab, v_ref, s_ref, k_ref, gs_ref, gk_ref, g):
    total = None
    for base, src in ((32, s_ref), (36, k_ref)):
        rows = [
            v_ref[pl.ds(pl.multiple_of(tab[base + i] * 128, 128), 128), :]
            for i in range(4)
        ]
        v = jnp.concatenate(rows, axis=0)
        part = dot3(split(v), split(src[...]), TN)
        total = part if total is None else total + part
    g[...] = total
    for base, out in ((32, gs_ref), (36, gk_ref)):
        for i in range(4):
            at = pl.ds(pl.multiple_of(tab[base + i] * 64, 64), 64)
            out[i * 64 : i * 64 + 64, :] = g[at, :]


def inner_product(tab, v, send, keep):
    return pl.pallas_call(
        inner_kernel,
        grid_spec=pltpu.PrefetchScalarGridSpec(
            num_scalar_prefetch=1,
            grid=(1,),
            in_specs=[full((1024, 512)), full((512, 512)), full((512, 512))],
            out_specs=[full((256, 512))] * 2,
            scratch_shapes=[pltpu.VMEM((512, 512), F32)],
        ),
        out_shape=[jax.ShapeDtypeStruct((256, 512), F32)] * 2,
        compiler_params=params(32),
        cost_estimate=cost(1024 * 512 * 512, 5 << 20),
    )(tab, v, send, keep)


def turned_kernel(tab, t_ref, v_ref, p0, p1, p2, p3, ch, cl, rh, rl, vh, vl):
    t = split(t_ref[...])
    place_blocks(tab, (p0, p1, p2, p3), vh, vl)
    for i in range(4):
        at = slice(i * 512, i * 512 + 512)
        ch[at, :], cl[at, :] = split(dot3((vh[at, :], vl[at, :]), t, NT))
    for i in range(2):
        at = slice(i * 512, i * 512 + 512)
        rh[at, :], rl[at, :] = split(dot3(split(v_ref[at, :]), t, NT))


def turned(tab, tfactor, v, pieces):
    return pl.pallas_call(
        turned_kernel,
        grid_spec=pltpu.PrefetchScalarGridSpec(
            num_scalar_prefetch=1,
            grid=(1,),
            in_specs=[full((512, 512)), full((1024, 512))] + [full((1024, 256))] * 4,
            out_specs=[full((2048, 512))] * 2 + [full((1024, 512))] * 2,
            scratch_shapes=[pltpu.VMEM((2048, 512), BF16)] * 2,
        ),
        out_shape=[jax.ShapeDtypeStruct((2048, 512), BF16)] * 2
        + [jax.ShapeDtypeStruct((1024, 512), BF16)] * 2,
        compiler_params=params(40),
        cost_estimate=cost(3072 * 512 * 512, 13 << 20),
    )(tab, tfactor, v, *pieces)


def place_cat(pieces, b3):
    for h, piece in enumerate(pieces):
        bh, bl = split(piece[...])
        b3[h, :, :256] = bh
        b3[h, :, 256:512] = bl
        b3[h, :, 512:] = bh


def less_blocks(tab, first, out, x, b3):
    for h in range(2):
        cols = slice(h * 256, h * 256 + 256)
        left = jnp.concatenate([x[0][:, cols], x[0][:, cols], x[1][:, cols]], axis=1)
        for p in range(4):
            right = b3[h, p * 256 : p * 256 + 256, :]
            part = lax.dot_general(left, right, NT, preferred_element_type=F32)
            for e in range(2):
                at = tab[h * 16 + first + p * 2 + e] * 128
                at = pl.ds(pl.multiple_of(at, 128), 128)
                out[:, at] = out[:, at] - part[:, e * 128 : e * 128 + 128]


def update_first_kernel(
    tab, a, p0, p1, wk, ws, gk, gs, rh, rl, ch, cl, out, b3, w, g, gh, gl
):
    step = pl.program_id(0)

    @pl.when(step == 0)
    def _():
        place_cat((p0, p1), b3)
        for base, gsrc, wsrc in ((36, gk, wk), (32, gs, ws)):
            for i in range(4):
                at = pl.ds(pl.multiple_of(tab[base + i] * 64, 64), 64)
                g[at, :] = gsrc[i * 64 : i * 64 + 64, :]
                at = pl.ds(pl.multiple_of(tab[base + i] * 128, 128), 128)
                w[at, :] = wsrc[i * 128 : i * 128 + 128, :]
        gh[...], gl[...] = split(g[...])

    x = (rh[...], rl[...])
    rows = pl.ds(pl.multiple_of(step * 256, 256), 256)
    left = split(w[rows, :] - dot3(x, (gh[...], gl[...]), NN))
    for i in range(4):
        at = slice(i * 512, i * 512 + 512)
        out[:, at] = a[:, at] - dot3(left, (ch[at, :], cl[at, :]), NT)
    less_blocks(tab, 0, out, x, b3)


def update_last_kernel(
    tab, a, p0, p1, rh, rl, b_ref, q0, q1, q2, q3, xh, xl, out, b_out,
    b3, qh, ql,
):
    step = pl.program_id(0)

    @pl.when(step == 0)
    def _():
        place_cat((p0, p1), b3)
        place_blocks(tab, (q0, q1, q2, q3), qh, ql, 32)

    out[...] = a[...]
    less_blocks(tab, 8, out, (rh[...], rl[...]), b3)
    rows = pl.ds(pl.multiple_of(step * 128, 128), 128)
    b_out[...] = b_ref[...] - dot3((qh[rows, :], ql[rows, :]), (xh[...], xl[...]), NT)


def update_first(tab, matrix, pieces, w_keep, w_other, g_keep, g_other, rh, rl, ch, cl):
    return pl.pallas_call(
        update_first_kernel,
        grid_spec=pltpu.PrefetchScalarGridSpec(
            num_scalar_prefetch=1,
            grid=(4,),
            in_specs=[tiled((256, 2048))]
            + [WHOLE] * 6
            + [tiled((256, 512))] * 2
            + [WHOLE] * 2,
            out_specs=tiled((256, 2048)),
            scratch_shapes=[pltpu.VMEM((2, 1024, 768), BF16)]
            + [pltpu.VMEM((1024, 512), F32), pltpu.VMEM((512, 512), F32)]
            + [pltpu.VMEM((512, 512), BF16)] * 2,
        ),
        out_shape=pltpu.HBM((1024, 2048), F32),
        compiler_params=params(26),
        cost_estimate=cost(7 * 1024 * 512 * 512, 26 << 20),
    )(
        tab, in_hbm(matrix),
        *[in_vmem(x) for x in (*pieces, w_keep, w_other, g_keep, g_other)],
        rh, rl, in_vmem(ch), in_vmem(cl),
    )


def update_last(tab, acc, pieces, basis, q_pieces, rh, rl):
    return pl.pallas_call(
        update_last_kernel,
        grid_spec=pltpu.PrefetchScalarGridSpec(
            num_scalar_prefetch=1,
            grid=(4,),
            in_specs=[tiled((256, 2048))]
            + [full((1024, 256))] * 2
            + [tiled((256, 512))] * 2
            + [tiled((128, 1024))]
            + [full((256, 256))] * 4
            + [full((1024, 512))] * 2,
            out_specs=[tiled((256, 2048)), tiled((128, 1024))],
            scratch_shapes=[pltpu.VMEM((2, 1024, 768), BF16)]
            + [pltpu.VMEM((512, 512), BF16)] * 2,
        ),
        out_shape=[
            jax.ShapeDtypeStruct((1024, 2048), F32),
            jax.ShapeDtypeStruct((512, 1024), F32),
        ],
        compiler_params=params(28),
        cost_estimate=cost(3 * 1024 * 512 * 512, 26 << 20),
    )(tab, in_hbm(acc), *pieces, rh, rl, in_hbm(basis), *q_pieces, rh, rl)


def on_device(matrix, basis_rows, reflectors, tfactor):
    dev = lax.axis_index(EVERY)
    tab = lax.dynamic_index_in_dim(jnp.asarray(TABLES), dev, 0, keepdims=False)
    member = lax.axis_index(("col", "grp"))
    own_v = lax.dynamic_slice_in_dim(reflectors, member * 128, 128, 0)

    q = list(basis_product(tab, basis_rows, reflectors))
    v = [own_v[:, :256], own_v[:, 256:]]
    last_v = [None, None]
    for s in range(4):
        messages = list(v)
        if s > 0:
            for h in range(2):
                half = q[h].shape[0] // 2
                messages[h] = jnp.concatenate([v[h], q[h][half:]], axis=0)
        messages = lax.optimization_barrier(messages)
        for h in range(2):
            n, half = v[h].shape[0], q[h].shape[0] // 2
            got = moved(messages[h], lambda c: row_dim(c, h, s))
            if s > 0:
                q[h] = q[h][:half] + got[n:]
            if s < 3:
                v[h] = jnp.concatenate([v[h], got[:n]], axis=0)
            else:
                last_v[h] = got[:n]

    partial = apply_matrix(tab, matrix, v)
    send, keep = apply_matrix(tab, matrix, last_v, partial)
    w = keep + moved(send, lambda c: "c")
    g_send, g_keep = inner_product(tab, reflectors, send, keep)
    g = g_keep + moved(g_send, lambda c: "c")
    w, g = w.reshape(4, 128, 512), g.reshape(4, 64, 512)
    ch, cl, rh, rl = turned(tab, tfactor, reflectors, (v[0], last_v[0], v[1], last_v[1]))
    for s in range(2):
        w = w.reshape(-1, 2, 128, 512)
        g = g.reshape(-1, 2, 64, 512)
        n = w.shape[0]
        message = jnp.concatenate(
            [w[:, 1].reshape(n * 128, 512), g[:, 1].reshape(n * 64, 512)], axis=0
        )
        if s == 1:
            message, ch, cl, rh, rl = lax.optimization_barrier((message, ch, cl, rh, rl))
        got = moved(message, lambda c: y_dim(c, s))
        w = w[:, 0] + got[: n * 128].reshape(n, 128, 512)
        g = g[:, 0] + got[n * 128 :].reshape(n, 64, 512)
    w, g = w.reshape(128, 512), g.reshape(64, 512)

    wc = [w[:, :256], w[:, 256:]]
    last_w, last_q = [None, None], [None, None]
    w_rows = w
    for s in range(4):
        g = g + moved(g, lambda c: row_dim(c, 0, s))
        for h in range(2):
            n = wc[h].shape[0]
            got = moved(
                jnp.concatenate([wc[h], q[h]], axis=0), lambda c: row_dim(c, h, s)
            )
            if s == 0:
                q[h] = q[h] + jnp.concatenate([got[n + 32 :], got[n : n + 32]], axis=0)
            elif s < 3:
                q[h] = jnp.concatenate([q[h], got[n:]], axis=0)
            else:
                last_q[h] = got[n:]
            if s < 3:
                wc[h] = jnp.concatenate([wc[h], got[:n]], axis=0)
            else:
                last_w[h] = got[:n]
        if s < 2:
            w_rows = jnp.concatenate(
                [w_rows, moved(w_rows, lambda c: y_dim(c, s))], axis=0
            )
    w_other = moved(w_rows, lambda c: "c")
    for s in range(2):
        g = jnp.concatenate([g, moved(g, lambda c: y_dim(c, s))], axis=0)
    g_other = moved(g, lambda c: "c")

    part = update_first(tab, matrix, wc, w_rows, w_other, g, g_other, rh, rl, ch, cl)
    q_pieces = (q[0], last_q[0], q[1], last_q[1])
    return tuple(update_last(tab, part, last_w, basis_rows, q_pieces, rh, rl))


def solution(mesh):
    placed = (P("row", ("col", "grp")), P(("col", "grp"), "row"), P("row", None), P())
    return jax.shard_map(
        on_device,
        mesh=mesh,
        in_specs=placed,
        out_specs=(P("row", ("col", "grp")), P(("col", "grp"), "row")),
        check_vma=False,
    )
```

```python
import jax
import jax.numpy as jnp
import numpy as np
from jax import lax
from jax.experimental import pallas as pl
from jax.experimental.pallas import tpu as pltpu
from jax.sharding import PartitionSpec as P

F32, BF16 = jnp.float32, jnp.bfloat16
EVERY = ("row", "col", "grp")
NN = (((1,), (0,)), ((), ()))
NT = (((1,), (1,)), ((), ()))
TN = (((0,), (0,)), ((), ()))


def flip_ring(i, bit):
    g = (i ^ (i >> 1)) ^ (1 << bit)
    return g ^ (g >> 1)


def linear(x, z, y, core):
    return (x * 4 + z) * 8 + ((y % 2) * 2 + core) * 2 + y // 2


def coords(dev):
    row, member = divmod(dev, 8)
    return row // 4, row % 4, (member % 2) * 2 + member // 4, (member // 2) % 2


def flip(dev, dim):
    x, z, y, core = coords(dev)
    if dim == "c":
        return linear(x, z, y, 1 - core)
    bit = int(dim[1])
    if dim[0] == "x":
        x = flip_ring(x, bit)
    elif dim[0] == "z":
        z = flip_ring(z, bit)
    else:
        y = flip_ring(y, bit)
    return linear(x, z, y, core)


ROW_DIMS = {
    (0, 0): ("x0", "z0", "x1", "z1"),
    (1, 0): ("z0", "x0", "z1", "x1"),
    (0, 1): ("x1", "z1", "x0", "z0"),
    (1, 1): ("z1", "x1", "z0", "x0"),
}


def row_dim(core, half, step):
    return ROW_DIMS[core, half][step]


def y_dim(core, step):
    return "y%d" % ((step + core) % 2)


def relative(dev, dims, j):
    for k, dim in enumerate(dims):
        if j >> k & 1:
            dev = flip(dev, dim)
    return dev


def build_tables():
    out = np.zeros((128, 64), np.int32)
    for dev in range(128):
        core = coords(dev)[3]
        for h in range(2):
            dims = [row_dim(core, h, s) for s in range(4)]
            for j in range(16):
                out[dev, h * 16 + j] = relative(dev, dims, j) // 8
        other = flip(dev, "c")
        for first, base in ((other, 32), (dev, 36)):
            dims = [y_dim(coords(first)[3], s) for s in range(2)]
            for j in range(4):
                out[dev, base + j] = relative(first, dims, j) % 8
        out[dev, 40] = dev % 8
    return out


TABLES = build_tables()


def moved(x, dim_of_core):
    pairs = [(dev, flip(dev, dim_of_core(coords(dev)[3]))) for dev in range(128)]
    return lax.ppermute(x, EVERY, pairs)


def split(x):
    hi = x.astype(BF16)
    return hi, (x - hi.astype(F32)).astype(BF16)


def dot3(a, b, dims):
    def one(u, v):
        return lax.dot_general(u, v, dims, preferred_element_type=F32)

    return one(a[0], b[0]) + (one(a[0], b[1]) + one(a[1], b[0]))


def cost(macs, moved_bytes):
    return pl.CostEstimate(flops=6 * macs, bytes_accessed=moved_bytes, transcendentals=0)


def params(mib):
    return pltpu.CompilerParams(vmem_limit_bytes=mib * 2**20)


def in_hbm(x):
    return pltpu.with_memory_space_constraint(x, pltpu.HBM)


def in_vmem(x):
    return pltpu.with_memory_space_constraint(x, pltpu.VMEM)


WHOLE = pl.BlockSpec(memory_space=pltpu.VMEM)


def full(shape):
    return pl.BlockSpec(shape, lambda *_: (0,) * len(shape))


def tiled(shape):
    return pl.BlockSpec(shape, lambda s, t: (s, 0))


def basis_kernel(tab, b_ref, v_ref, q0_ref, q1_ref, q):
    q[...] = dot3(split(b_ref[...]), split(v_ref[...]), NN)
    for h, out in enumerate((q0_ref, q1_ref)):
        for j in range(16):
            place = (j >> 1 & 1) * 8 + (j >> 2 & 1) * 4 + (j >> 3 & 1) * 2 + (j & 1)
            rows = pl.ds(pl.multiple_of(tab[h * 16 + j] * 32, 32), 32)
            out[place * 32 : place * 32 + 32, :] = q[rows, h * 256 : h * 256 + 256]


def basis_product(tab, basis, v):
    return pl.pallas_call(
        basis_kernel,
        grid_spec=pltpu.PrefetchScalarGridSpec(
            num_scalar_prefetch=1,
            grid=(1,),
            in_specs=[full((512, 1024)), full((1024, 512))],
            out_specs=[full((512, 256))] * 2,
            scratch_shapes=[pltpu.VMEM((512, 512), F32)],
        ),
        out_shape=[jax.ShapeDtypeStruct((512, 256), F32)] * 2,
        compiler_params=params(32),
        cost_estimate=cost(512 * 1024 * 512, 5 << 20),
    )(tab, in_hbm(basis), in_hbm(v))


def place_blocks(tab, pieces, hi, lo, rows=128):
    for h in range(2):
        for j in range(16):
            src = pieces[h * 2 + j // 8]
            block = src[(j % 8) * rows : (j % 8) * rows + rows, :]
            bh, bl = split(block)
            at = pl.ds(pl.multiple_of(tab[h * 16 + j] * rows, rows), rows)
            hi[at, h * 256 : h * 256 + 256] = bh
            lo[at, h * 256 : h * 256 + 256] = bl


def apply_part(tab, first, a_refs, pieces, ah, al, vh, vl, out, add):
    @pl.when(pl.program_id(0) == 0)
    def _():
        for h in range(2):
            vh[h], vl[h] = split(pieces[h][...])

    for h in range(2):
        for i, a in enumerate(a_refs):
            for j in range(8):
                at = tab[h * 16 + first + j] * 128
                block = a[:, pl.ds(pl.multiple_of(at, 128), 128)]
                rows, lanes = slice(i * 128, i * 128 + 128), slice(j * 128, j * 128 + 128)
                ah[rows, lanes], al[rows, lanes] = split(block)
        part = dot3((ah[...], al[...]), (vh[h], vl[h]), NN)
        lanes = slice(h * 256, h * 256 + 256)
        out[:, lanes] = part if add is None else part + add[:, lanes]


def apply_first_kernel(tab, a0, a1, a2, a3, p0, p1, out, ah, al, vh, vl):
    apply_part(tab, 0, (a0, a1, a2, a3), (p0, p1), ah, al, vh, vl, out, None)


def apply_last_kernel(tab, a0, a1, a2, a3, p0, p1, acc, send, keep, ah, al, vh, vl):
    for s, out in enumerate((send, keep)):

        @pl.when(pl.program_id(0) == s)
        def _(out=out):
            apply_part(tab, 8, (a0, a1, a2, a3), (p0, p1), ah, al, vh, vl, out, acc)


def apply_matrix(tab, matrix, pieces, acc=None):
    def a_spec(i):
        return pl.BlockSpec((128, 2048), lambda s, t, i=i: (t[32 + s * 4 + i], 0))

    tile = pl.BlockSpec((512, 512), lambda s, t: (s, 0))
    last = acc is not None
    return pl.pallas_call(
        apply_last_kernel if last else apply_first_kernel,
        grid_spec=pltpu.PrefetchScalarGridSpec(
            num_scalar_prefetch=1,
            grid=(2,),
            in_specs=[a_spec(i) for i in range(4)]
            + [full((1024, 256))] * 2
            + [tile] * last,
            out_specs=[full((512, 512))] * 2 if last else tile,
            scratch_shapes=[pltpu.VMEM((512, 1024), BF16)] * 2
            + [pltpu.VMEM((2, 1024, 256), BF16)] * 2,
        ),
        out_shape=[jax.ShapeDtypeStruct((512, 512), F32)] * 2
        if last
        else jax.ShapeDtypeStruct((1024, 512), F32),
        compiler_params=params(28),
        cost_estimate=cost(1024 * 1024 * 512, 12 << 20),
    )(tab, *[matrix] * 4, *pieces, *([acc] if last else []))


def inner_kernel(tab, v_ref, s_ref, k_ref, gs_ref, gk_ref, g):
    total = None
    for base, src in ((32, s_ref), (36, k_ref)):
        rows = [
            v_ref[pl.ds(pl.multiple_of(tab[base + i] * 128, 128), 128), :]
            for i in range(4)
        ]
        v = jnp.concatenate(rows, axis=0)
        part = dot3(split(v), split(src[...]), TN)
        total = part if total is None else total + part
    g[...] = total
    for base, out in ((32, gs_ref), (36, gk_ref)):
        for i in range(4):
            at = pl.ds(pl.multiple_of(tab[base + i] * 64, 64), 64)
            out[i * 64 : i * 64 + 64, :] = g[at, :]


def inner_product(tab, v, send, keep):
    return pl.pallas_call(
        inner_kernel,
        grid_spec=pltpu.PrefetchScalarGridSpec(
            num_scalar_prefetch=1,
            grid=(1,),
            in_specs=[full((1024, 512)), full((512, 512)), full((512, 512))],
            out_specs=[full((256, 512))] * 2,
            scratch_shapes=[pltpu.VMEM((512, 512), F32)],
        ),
        out_shape=[jax.ShapeDtypeStruct((256, 512), F32)] * 2,
        compiler_params=params(32),
        cost_estimate=cost(1024 * 512 * 512, 5 << 20),
    )(tab, v, send, keep)


def turned_kernel(tab, t_ref, v_ref, p0, p1, p2, p3, ch, cl, rh, rl, vh, vl):
    t = split(t_ref[...])
    place_blocks(tab, (p0, p1, p2, p3), vh, vl)
    for i in range(4):
        at = slice(i * 512, i * 512 + 512)
        ch[at, :], cl[at, :] = split(dot3((vh[at, :], vl[at, :]), t, NT))
    for i in range(2):
        at = slice(i * 512, i * 512 + 512)
        rh[at, :], rl[at, :] = split(dot3(split(v_ref[at, :]), t, NT))


def turned(tab, tfactor, v, pieces):
    return pl.pallas_call(
        turned_kernel,
        grid_spec=pltpu.PrefetchScalarGridSpec(
            num_scalar_prefetch=1,
            grid=(1,),
            in_specs=[full((512, 512)), full((1024, 512))] + [full((1024, 256))] * 4,
            out_specs=[full((2048, 512))] * 2 + [full((1024, 512))] * 2,
            scratch_shapes=[pltpu.VMEM((2048, 512), BF16)] * 2,
        ),
        out_shape=[jax.ShapeDtypeStruct((2048, 512), BF16)] * 2
        + [jax.ShapeDtypeStruct((1024, 512), BF16)] * 2,
        compiler_params=params(40),
        cost_estimate=cost(3072 * 512 * 512, 13 << 20),
    )(tab, tfactor, v, *pieces)


def place_cat(pieces, b3):
    for h, piece in enumerate(pieces):
        bh, bl = split(piece[...])
        b3[h, :, :256] = bh
        b3[h, :, 256:512] = bl
        b3[h, :, 512:] = bh


def less_blocks(tab, first, src, src_rows, out, rows, x, b3, part):
    for h in range(2):
        cols = slice(h * 256, h * 256 + 256)
        left = jnp.concatenate([x[0][:, cols], x[0][:, cols], x[1][:, cols]], axis=1)
        part[h] = lax.dot_general(left, b3[h], NT, preferred_element_type=F32)
    for h in range(2):
        for j in range(8):
            at = tab[h * 16 + first + j] * 128
            at = pl.ds(pl.multiple_of(at, 128), 128)
            old = src[src_rows, at] if h == 0 else out[rows, at]
            out[rows, at] = old - part[h, :, j * 128 : j * 128 + 128]
        if h == 0 and src is not out:
            for j in range(8):
                at = tab[(first + j + 8) % 16] * 128
                at = pl.ds(pl.multiple_of(at, 128), 128)
                out[rows, at] = src[src_rows, at]


def update_first_kernel(
    tab, a, p0, p1, wk, ws, gk, gs, rh, rl, ch, cl, out, b3, part, w, g, gh, gl
):
    step = pl.program_id(0)

    @pl.when(step == 0)
    def _():
        place_cat((p0, p1), b3)
        for base, gsrc, wsrc in ((36, gk, wk), (32, gs, ws)):
            for i in range(4):
                at = pl.ds(pl.multiple_of(tab[base + i] * 64, 64), 64)
                g[at, :] = gsrc[i * 64 : i * 64 + 64, :]
                at = pl.ds(pl.multiple_of(tab[base + i] * 128, 128), 128)
                w[at, :] = wsrc[i * 128 : i * 128 + 128, :]
        gh[...], gl[...] = split(g[...])

    x = (rh[...], rl[...])
    rows = pl.ds(pl.multiple_of(step * 256, 256), 256)
    left = split(w[rows, :] - dot3(x, (gh[...], gl[...]), NN))
    for i in range(4):
        at = slice(i * 512, i * 512 + 512)
        out[rows, at] = a[:, at] - dot3(left, (ch[at, :], cl[at, :]), NT)
    less_blocks(tab, 0, out, rows, out, rows, x, b3, part)


def update_last_kernel(
    tab, a, p0, p1, rh, rl, b_ref, q0, q1, q2, q3, xh, xl, out, b_out,
    b3, part, qh, ql,
):
    step = pl.program_id(0)

    @pl.when(step == 0)
    def _():
        place_cat((p0, p1), b3)
        place_blocks(tab, (q0, q1, q2, q3), qh, ql, 32)

    acc_rows = pl.ds(pl.multiple_of(step * 256, 256), 256)
    x = (rh[...], rl[...])
    less_blocks(tab, 8, a, acc_rows, out, slice(None), x, b3, part)
    rows = pl.ds(pl.multiple_of(step * 128, 128), 128)
    b_out[...] = b_ref[...] - dot3((qh[rows, :], ql[rows, :]), (xh[...], xl[...]), NT)


def update_first(tab, matrix, pieces, w_keep, w_other, g_keep, g_other, rh, rl, ch, cl):
    return pl.pallas_call(
        update_first_kernel,
        grid_spec=pltpu.PrefetchScalarGridSpec(
            num_scalar_prefetch=1,
            grid=(4,),
            in_specs=[tiled((256, 2048))]
            + [WHOLE] * 6
            + [tiled((256, 512))] * 2
            + [WHOLE] * 2,
            out_specs=WHOLE,
            scratch_shapes=[pltpu.VMEM((2, 1024, 768), BF16), pltpu.VMEM((2, 256, 1024), F32)]
            + [pltpu.VMEM((1024, 512), F32), pltpu.VMEM((512, 512), F32)]
            + [pltpu.VMEM((512, 512), BF16)] * 2,
        ),
        out_shape=pltpu.VMEM((1024, 2048), F32),
        compiler_params=params(24),
        cost_estimate=cost(7 * 1024 * 512 * 512, 26 << 20),
    )(
        tab, in_hbm(matrix),
        *[in_vmem(x) for x in (*pieces, w_keep, w_other, g_keep, g_other)],
        rh, rl, in_vmem(ch), in_vmem(cl),
    )


def update_last(tab, acc, pieces, basis, q_pieces, rh, rl):
    return pl.pallas_call(
        update_last_kernel,
        grid_spec=pltpu.PrefetchScalarGridSpec(
            num_scalar_prefetch=1,
            grid=(4,),
            in_specs=[WHOLE] * 3
            + [tiled((256, 512))] * 2
            + [tiled((128, 1024))]
            + [WHOLE] * 6,
            out_specs=[tiled((256, 2048)), tiled((128, 1024))],
            scratch_shapes=[pltpu.VMEM((2, 1024, 768), BF16), pltpu.VMEM((2, 256, 1024), F32)]
            + [pltpu.VMEM((512, 512), BF16)] * 2,
        ),
        out_shape=[
            jax.ShapeDtypeStruct((1024, 2048), F32),
            jax.ShapeDtypeStruct((512, 1024), F32),
        ],
        compiler_params=params(20),
        cost_estimate=cost(3 * 1024 * 512 * 512, 26 << 20),
    )(
        tab, *[in_vmem(x) for x in (acc, *pieces)],
        rh, rl, in_hbm(basis),
        *[in_vmem(x) for x in (*q_pieces, rh, rl)],
    )


def on_device(matrix, basis_rows, reflectors, tfactor):
    dev = lax.axis_index(EVERY)
    tab = lax.dynamic_index_in_dim(jnp.asarray(TABLES), dev, 0, keepdims=False)
    member = lax.axis_index(("col", "grp"))
    own_v = lax.dynamic_slice_in_dim(reflectors, member * 128, 128, 0)

    q = list(basis_product(tab, basis_rows, reflectors))
    v = [own_v[:, :256], own_v[:, 256:]]
    last_v = [None, None]
    for s in range(4):
        messages = list(v)
        if s > 0:
            for h in range(2):
                half = q[h].shape[0] // 2
                messages[h] = jnp.concatenate([v[h], q[h][half:]], axis=0)
        messages = lax.optimization_barrier(messages)
        for h in range(2):
            n, half = v[h].shape[0], q[h].shape[0] // 2
            got = moved(messages[h], lambda c: row_dim(c, h, s))
            if s > 0:
                q[h] = q[h][:half] + got[n:]
            if s < 3:
                v[h] = jnp.concatenate([v[h], got[:n]], axis=0)
            else:
                last_v[h] = got[:n]

    partial = apply_matrix(tab, matrix, v)
    send, keep = apply_matrix(tab, matrix, last_v, partial)
    w = keep + moved(send, lambda c: "c")
    g_send, g_keep = inner_product(tab, reflectors, send, keep)
    g = g_keep + moved(g_send, lambda c: "c")
    w, g = w.reshape(4, 128, 512), g.reshape(4, 64, 512)
    ch, cl, rh, rl = turned(tab, tfactor, reflectors, (v[0], last_v[0], v[1], last_v[1]))
    for s in range(2):
        w = w.reshape(-1, 2, 128, 512)
        g = g.reshape(-1, 2, 64, 512)
        n = w.shape[0]
        message = jnp.concatenate(
            [w[:, 1].reshape(n * 128, 512), g[:, 1].reshape(n * 64, 512)], axis=0
        )
        if s == 1:
            message, ch, cl, rh, rl = lax.optimization_barrier((message, ch, cl, rh, rl))
        got = moved(message, lambda c: y_dim(c, s))
        w = w[:, 0] + got[: n * 128].reshape(n, 128, 512)
        g = g[:, 0] + got[n * 128 :].reshape(n, 64, 512)
    w, g = w.reshape(128, 512), g.reshape(64, 512)

    wc = [w[:, :256], w[:, 256:]]
    last_w, last_q = [None, None], [None, None]
    w_rows = w
    for s in range(4):
        g = g + moved(g, lambda c: row_dim(c, 0, s))
        for h in range(2):
            n = wc[h].shape[0]
            got = moved(
                jnp.concatenate([wc[h], q[h]], axis=0), lambda c: row_dim(c, h, s)
            )
            if s == 0:
                q[h] = q[h] + jnp.concatenate([got[n + 32 :], got[n : n + 32]], axis=0)
            elif s < 3:
                q[h] = jnp.concatenate([q[h], got[n:]], axis=0)
            else:
                last_q[h] = got[n:]
            if s < 3:
                wc[h] = jnp.concatenate([wc[h], got[:n]], axis=0)
            else:
                last_w[h] = got[:n]
        if s < 2:
            w_rows = jnp.concatenate(
                [w_rows, moved(w_rows, lambda c: y_dim(c, s))], axis=0
            )
    w_other = moved(w_rows, lambda c: "c")
    for s in range(2):
        g = jnp.concatenate([g, moved(g, lambda c: y_dim(c, s))], axis=0)
    g_other = moved(g, lambda c: "c")

    part = update_first(tab, matrix, wc, w_rows, w_other, g, g_other, rh, rl, ch, cl)
    q_pieces = (q[0], last_q[0], q[1], last_q[1])
    return tuple(update_last(tab, part, last_w, basis_rows, q_pieces, rh, rl))


def solution(mesh):
    placed = (P("row", ("col", "grp")), P(("col", "grp"), "row"), P("row", None), P())
    return jax.shard_map(
        on_device,
        mesh=mesh,
        in_specs=placed,
        out_specs=(P("row", ("col", "grp")), P(("col", "grp"), "row")),
        check_vma=False,
    )
```

```python
import jax
import jax.numpy as jnp
import numpy as np
from jax import lax
from jax.experimental import pallas as pl
from jax.experimental.pallas import tpu as pltpu
from jax.sharding import PartitionSpec as P

F32, BF16 = jnp.float32, jnp.bfloat16
EVERY = ("row", "col", "grp")
NN = (((1,), (0,)), ((), ()))
NT = (((1,), (1,)), ((), ()))
TN = (((0,), (0,)), ((), ()))


def flip_ring(i, bit):
    g = (i ^ (i >> 1)) ^ (1 << bit)
    return g ^ (g >> 1)


def linear(x, z, y, core):
    return (x * 4 + z) * 8 + ((y % 2) * 2 + core) * 2 + y // 2


def coords(dev):
    row, member = divmod(dev, 8)
    return row // 4, row % 4, (member % 2) * 2 + member // 4, (member // 2) % 2


def flip(dev, dim):
    x, z, y, core = coords(dev)
    if dim == "c":
        return linear(x, z, y, 1 - core)
    bit = int(dim[1])
    if dim[0] == "x":
        x = flip_ring(x, bit)
    elif dim[0] == "z":
        z = flip_ring(z, bit)
    else:
        y = flip_ring(y, bit)
    return linear(x, z, y, core)


ROW_DIMS = {
    (0, 0): ("x0", "z0", "x1", "z1"),
    (1, 0): ("z0", "x0", "z1", "x1"),
    (0, 1): ("x1", "z1", "x0", "z0"),
    (1, 1): ("z1", "x1", "z0", "x0"),
}


def row_dim(core, half, step):
    return ROW_DIMS[core, half][step]


def y_dim(core, step):
    return "y%d" % ((step + core) % 2)


def relative(dev, dims, j):
    for k, dim in enumerate(dims):
        if j >> k & 1:
            dev = flip(dev, dim)
    return dev


def build_tables():
    out = np.zeros((128, 64), np.int32)
    for dev in range(128):
        core = coords(dev)[3]
        for h in range(2):
            dims = [row_dim(core, h, s) for s in range(4)]
            for j in range(16):
                out[dev, h * 16 + j] = relative(dev, dims, j) // 8
        other = flip(dev, "c")
        for first, base in ((other, 32), (dev, 36)):
            dims = [y_dim(coords(first)[3], s) for s in range(2)]
            for j in range(4):
                out[dev, base + j] = relative(first, dims, j) % 8
        out[dev, 40] = dev % 8
    return out


TABLES = build_tables()


def moved(x, dim_of_core):
    pairs = [(dev, flip(dev, dim_of_core(coords(dev)[3]))) for dev in range(128)]
    return lax.ppermute(x, EVERY, pairs)


def split(x):
    hi = x.astype(BF16)
    return hi, (x - hi.astype(F32)).astype(BF16)


def dot3(a, b, dims):
    def one(u, v):
        return lax.dot_general(u, v, dims, preferred_element_type=F32)

    return one(a[0], b[0]) + (one(a[0], b[1]) + one(a[1], b[0]))


def cost(macs, moved_bytes):
    return pl.CostEstimate(flops=6 * macs, bytes_accessed=moved_bytes, transcendentals=0)


def params(mib):
    return pltpu.CompilerParams(vmem_limit_bytes=mib * 2**20)


def in_hbm(x):
    return pltpu.with_memory_space_constraint(x, pltpu.HBM)


def in_vmem(x):
    return pltpu.with_memory_space_constraint(x, pltpu.VMEM)


WHOLE = pl.BlockSpec(memory_space=pltpu.VMEM)


def full(shape):
    return pl.BlockSpec(shape, lambda *_: (0,) * len(shape))


def tiled(shape):
    return pl.BlockSpec(shape, lambda s, t: (s, 0))


def basis_kernel(tab, b_ref, v_ref, q0_ref, q1_ref, q):
    q[...] = dot3(split(b_ref[...]), split(v_ref[...]), NN)
    for h, out in enumerate((q0_ref, q1_ref)):
        for j in range(16):
            place = (j >> 1 & 1) * 8 + (j >> 2 & 1) * 4 + (j >> 3 & 1) * 2 + (j & 1)
            rows = pl.ds(pl.multiple_of(tab[h * 16 + j] * 32, 32), 32)
            out[place * 32 : place * 32 + 32, :] = q[rows, h * 256 : h * 256 + 256]


def basis_product(tab, basis, v):
    return pl.pallas_call(
        basis_kernel,
        grid_spec=pltpu.PrefetchScalarGridSpec(
            num_scalar_prefetch=1,
            grid=(1,),
            in_specs=[full((512, 1024)), full((1024, 512))],
            out_specs=[full((512, 256))] * 2,
            scratch_shapes=[pltpu.VMEM((512, 512), F32)],
        ),
        out_shape=[jax.ShapeDtypeStruct((512, 256), F32)] * 2,
        compiler_params=params(32),
        cost_estimate=cost(512 * 1024 * 512, 5 << 20),
    )(tab, in_hbm(basis), in_hbm(v))


def place_blocks(tab, pieces, hi, lo, rows=128):
    for h in range(2):
        for j in range(16):
            src = pieces[h * 2 + j // 8]
            block = src[(j % 8) * rows : (j % 8) * rows + rows, :]
            bh, bl = split(block)
            at = pl.ds(pl.multiple_of(tab[h * 16 + j] * rows, rows), rows)
            hi[at, h * 256 : h * 256 + 256] = bh
            lo[at, h * 256 : h * 256 + 256] = bl


def apply_part(tab, first, a_refs, pieces, ah, al, vh, vl, out, add):
    @pl.when(pl.program_id(0) == 0)
    def _():
        for h in range(2):
            vh[h], vl[h] = split(pieces[h][...])

    for h in range(2):
        for i, a in enumerate(a_refs):
            for j in range(8):
                at = tab[h * 16 + first + j] * 128
                block = a[:, pl.ds(pl.multiple_of(at, 128), 128)]
                rows, lanes = slice(i * 128, i * 128 + 128), slice(j * 128, j * 128 + 128)
                ah[rows, lanes], al[rows, lanes] = split(block)
        part = dot3((ah[...], al[...]), (vh[h], vl[h]), NN)
        lanes = slice(h * 256, h * 256 + 256)
        out[:, lanes] = part if add is None else part + add[:, lanes]


def apply_first_kernel(tab, a0, a1, a2, a3, p0, p1, out, ah, al, vh, vl):
    apply_part(tab, 0, (a0, a1, a2, a3), (p0, p1), ah, al, vh, vl, out, None)


def apply_last_kernel(tab, a0, a1, a2, a3, p0, p1, acc, send, keep, ah, al, vh, vl):
    for s, out in enumerate((send, keep)):

        @pl.when(pl.program_id(0) == s)
        def _(out=out):
            apply_part(tab, 8, (a0, a1, a2, a3), (p0, p1), ah, al, vh, vl, out, acc)


def apply_matrix(tab, matrix, pieces, acc=None):
    def a_spec(i):
        return pl.BlockSpec((128, 2048), lambda s, t, i=i: (t[32 + s * 4 + i], 0))

    tile = pl.BlockSpec((512, 512), lambda s, t: (s, 0))
    last = acc is not None
    return pl.pallas_call(
        apply_last_kernel if last else apply_first_kernel,
        grid_spec=pltpu.PrefetchScalarGridSpec(
            num_scalar_prefetch=1,
            grid=(2,),
            in_specs=[a_spec(i) for i in range(4)]
            + [full((1024, 256))] * 2
            + [tile] * last,
            out_specs=[full((512, 512))] * 2 if last else tile,
            scratch_shapes=[pltpu.VMEM((512, 1024), BF16)] * 2
            + [pltpu.VMEM((2, 1024, 256), BF16)] * 2,
        ),
        out_shape=[jax.ShapeDtypeStruct((512, 512), F32)] * 2
        if last
        else jax.ShapeDtypeStruct((1024, 512), F32),
        compiler_params=params(28),
        cost_estimate=cost(1024 * 1024 * 512, 12 << 20),
    )(tab, *[matrix] * 4, *pieces, *([acc] if last else []))


def inner_kernel(tab, v_ref, s_ref, k_ref, gs_ref, gk_ref, g):
    total = None
    for base, src in ((32, s_ref), (36, k_ref)):
        rows = [
            v_ref[pl.ds(pl.multiple_of(tab[base + i] * 128, 128), 128), :]
            for i in range(4)
        ]
        v = jnp.concatenate(rows, axis=0)
        part = dot3(split(v), split(src[...]), TN)
        total = part if total is None else total + part
    g[...] = total
    for base, out in ((32, gs_ref), (36, gk_ref)):
        for i in range(4):
            at = pl.ds(pl.multiple_of(tab[base + i] * 64, 64), 64)
            out[i * 64 : i * 64 + 64, :] = g[at, :]


def inner_product(tab, v, send, keep):
    return pl.pallas_call(
        inner_kernel,
        grid_spec=pltpu.PrefetchScalarGridSpec(
            num_scalar_prefetch=1,
            grid=(1,),
            in_specs=[full((1024, 512)), full((512, 512)), full((512, 512))],
            out_specs=[full((256, 512))] * 2,
            scratch_shapes=[pltpu.VMEM((512, 512), F32)],
        ),
        out_shape=[jax.ShapeDtypeStruct((256, 512), F32)] * 2,
        compiler_params=params(32),
        cost_estimate=cost(1024 * 512 * 512, 5 << 20),
    )(tab, v, send, keep)


def turned_kernel(tab, t_ref, v_ref, p0, p1, p2, p3, ch, cl, rh, rl, vh, vl):
    t = split(t_ref[...])
    place_blocks(tab, (p0, p1, p2, p3), vh, vl)
    for i in range(4):
        at = slice(i * 512, i * 512 + 512)
        ch[at, :], cl[at, :] = split(dot3((vh[at, :], vl[at, :]), t, NT))
    for i in range(2):
        at = slice(i * 512, i * 512 + 512)
        rh[at, :], rl[at, :] = split(dot3(split(v_ref[at, :]), t, NT))


def turned(tab, tfactor, v, pieces):
    return pl.pallas_call(
        turned_kernel,
        grid_spec=pltpu.PrefetchScalarGridSpec(
            num_scalar_prefetch=1,
            grid=(1,),
            in_specs=[full((512, 512)), full((1024, 512))] + [full((1024, 256))] * 4,
            out_specs=[full((2048, 512))] * 2 + [full((1024, 512))] * 2,
            scratch_shapes=[pltpu.VMEM((2048, 512), BF16)] * 2,
        ),
        out_shape=[jax.ShapeDtypeStruct((2048, 512), BF16)] * 2
        + [jax.ShapeDtypeStruct((1024, 512), BF16)] * 2,
        compiler_params=params(40),
        cost_estimate=cost(3072 * 512 * 512, 13 << 20),
    )(tab, tfactor, v, *pieces)


def place_cat(pieces, b3):
    for h, piece in enumerate(pieces):
        bh, bl = split(piece[...])
        b3[h, :, :256] = bh
        b3[h, :, 256:512] = bl
        b3[h, :, 512:] = bh


def less_blocks(tab, first, src, src_rows, out, rows, x, b3, part):
    for h in range(2):
        cols = slice(h * 256, h * 256 + 256)
        left = jnp.concatenate([x[0][:, cols], x[0][:, cols], x[1][:, cols]], axis=1)
        part[h] = lax.dot_general(left, b3[h], NT, preferred_element_type=F32)
    for h in range(2):
        for j in range(8):
            at = tab[h * 16 + first + j] * 128
            at = pl.ds(pl.multiple_of(at, 128), 128)
            old = src[src_rows, at] if h == 0 else out[rows, at]
            out[rows, at] = old - part[h, :, j * 128 : j * 128 + 128]
        if h == 0 and src is not out:
            for j in range(8):
                at = tab[(first + j + 8) % 16] * 128
                at = pl.ds(pl.multiple_of(at, 128), 128)
                out[rows, at] = src[src_rows, at]


def update_first_kernel(
    tab, a, p0, p1, wk, ws, gk, gs, rh, rl, ch, cl, out, b3, part, w, g, gh, gl
):
    step = pl.program_id(0)

    @pl.when(step == 0)
    def _():
        place_cat((p0, p1), b3)
        for base, gsrc, wsrc in ((36, gk, wk), (32, gs, ws)):
            for i in range(4):
                at = tab[base + (0, 2, 1, 3)[i]] * 64
                at = pl.ds(pl.multiple_of(at, 64), 64)
                g[at, :] = gsrc[i * 64 : i * 64 + 64, :]
                at = pl.ds(pl.multiple_of(tab[base + i] * 128, 128), 128)
                w[at, :] = wsrc[i * 128 : i * 128 + 128, :]
        gh[...], gl[...] = split(g[...])

    x = (rh[...], rl[...])
    rows = pl.ds(pl.multiple_of(step * 256, 256), 256)
    left = split(w[rows, :] - dot3(x, (gh[...], gl[...]), NN))
    for i in range(4):
        at = slice(i * 512, i * 512 + 512)
        out[rows, at] = a[:, at] - dot3(left, (ch[at, :], cl[at, :]), NT)
    less_blocks(tab, 0, out, rows, out, rows, x, b3, part)


def update_last_kernel(
    tab, a, p0, p1, rh, rl, b_ref, q0, q1, q2, q3, xh, xl, out, b_out,
    b3, part, qh, ql,
):
    step = pl.program_id(0)

    @pl.when(step == 0)
    def _():
        place_cat((p0, p1), b3)
        place_blocks(tab, (q0, q1, q2, q3), qh, ql, 32)

    acc_rows = pl.ds(pl.multiple_of(step * 256, 256), 256)
    x = (rh[...], rl[...])
    less_blocks(tab, 8, a, acc_rows, out, slice(None), x, b3, part)
    rows = pl.ds(pl.multiple_of(step * 128, 128), 128)
    b_out[...] = b_ref[...] - dot3((qh[rows, :], ql[rows, :]), (xh[...], xl[...]), NT)


def update_first(tab, matrix, pieces, w_keep, w_other, g_keep, g_other, rh, rl, ch, cl):
    return pl.pallas_call(
        update_first_kernel,
        grid_spec=pltpu.PrefetchScalarGridSpec(
            num_scalar_prefetch=1,
            grid=(4,),
            in_specs=[tiled((256, 2048))]
            + [WHOLE] * 6
            + [tiled((256, 512))] * 2
            + [WHOLE] * 2,
            out_specs=WHOLE,
            scratch_shapes=[pltpu.VMEM((2, 1024, 768), BF16), pltpu.VMEM((2, 256, 1024), F32)]
            + [pltpu.VMEM((1024, 512), F32), pltpu.VMEM((512, 512), F32)]
            + [pltpu.VMEM((512, 512), BF16)] * 2,
        ),
        out_shape=pltpu.VMEM((1024, 2048), F32),
        compiler_params=params(24),
        cost_estimate=cost(7 * 1024 * 512 * 512, 26 << 20),
    )(
        tab, in_hbm(matrix),
        *[in_vmem(x) for x in (*pieces, w_keep, w_other, g_keep, g_other)],
        rh, rl, in_vmem(ch), in_vmem(cl),
    )


def update_last(tab, acc, pieces, basis, q_pieces, rh, rl):
    return pl.pallas_call(
        update_last_kernel,
        grid_spec=pltpu.PrefetchScalarGridSpec(
            num_scalar_prefetch=1,
            grid=(4,),
            in_specs=[WHOLE] * 3
            + [tiled((256, 512))] * 2
            + [tiled((128, 1024))]
            + [WHOLE] * 6,
            out_specs=[tiled((256, 2048)), tiled((128, 1024))],
            scratch_shapes=[pltpu.VMEM((2, 1024, 768), BF16), pltpu.VMEM((2, 256, 1024), F32)]
            + [pltpu.VMEM((512, 512), BF16)] * 2,
        ),
        out_shape=[
            jax.ShapeDtypeStruct((1024, 2048), F32),
            jax.ShapeDtypeStruct((512, 1024), F32),
        ],
        compiler_params=params(20),
        cost_estimate=cost(3 * 1024 * 512 * 512, 26 << 20),
    )(
        tab, *[in_vmem(x) for x in (acc, *pieces)],
        rh, rl, in_hbm(basis),
        *[in_vmem(x) for x in (*q_pieces, rh, rl)],
    )


def on_device(matrix, basis_rows, reflectors, tfactor):
    dev = lax.axis_index(EVERY)
    tab = lax.dynamic_index_in_dim(jnp.asarray(TABLES), dev, 0, keepdims=False)
    member = lax.axis_index(("col", "grp"))
    own_v = lax.dynamic_slice_in_dim(reflectors, member * 128, 128, 0)

    q = list(basis_product(tab, basis_rows, reflectors))
    v = [own_v[:, :256], own_v[:, 256:]]
    last_v = [None, None]
    for s in range(4):
        messages = list(v)
        if s > 0:
            for h in range(2):
                half = q[h].shape[0] // 2
                messages[h] = jnp.concatenate([v[h], q[h][half:]], axis=0)
        messages = lax.optimization_barrier(messages)
        for h in range(2):
            n, half = v[h].shape[0], q[h].shape[0] // 2
            got = moved(messages[h], lambda c: row_dim(c, h, s))
            if s > 0:
                q[h] = q[h][:half] + got[n:]
            if s < 3:
                v[h] = jnp.concatenate([v[h], got[:n]], axis=0)
            else:
                last_v[h] = got[:n]

    partial = apply_matrix(tab, matrix, v)
    send, keep = apply_matrix(tab, matrix, last_v, partial)
    w = keep + moved(send, lambda c: "c")
    g_send, g_keep = inner_product(tab, reflectors, send, keep)
    g = g_keep + moved(g_send, lambda c: "c")
    w, g = w.reshape(4, 128, 512), g.reshape(4, 64, 512)
    ch, cl, rh, rl = turned(tab, tfactor, reflectors, (v[0], last_v[0], v[1], last_v[1]))
    message = jnp.concatenate(
        [w[1::2].reshape(256, 512), g[1::2].reshape(128, 512)], axis=0
    )
    got = moved(message, lambda c: y_dim(c, 0))
    w = w[::2].reshape(256, 512) + got[:256]
    g = g[::2].reshape(128, 512) + got[256:]
    w, g, ch, cl, rh, rl = lax.optimization_barrier((w, g, ch, cl, rh, rl))
    w = w[:128] + moved(w[128:], lambda c: y_dim(c, 1))
    g = g + moved(g, lambda c: row_dim(c, 0, 3))

    wc = [w[:, :256], w[:, 256:]]
    last_w, last_q = [None, None], [None, None]
    w_rows = w
    for s in range(4):
        messages = [jnp.concatenate([wc[h], q[h]], axis=0) for h in range(2)]
        if s < 2:
            m0, m1, g, w_rows = lax.optimization_barrier((*messages, g, w_rows))
        else:
            m0, m1 = lax.optimization_barrier(messages)
        for h, message in enumerate((m0, m1)):
            n = wc[h].shape[0]
            got = moved(message, lambda c: row_dim(c, h, s))
            if s == 0:
                q[h] = q[h] + jnp.concatenate([got[n + 32 :], got[n : n + 32]], axis=0)
            elif s < 3:
                q[h] = jnp.concatenate([q[h], got[n:]], axis=0)
            else:
                last_q[h] = got[n:]
            if s < 3:
                wc[h] = jnp.concatenate([wc[h], got[:n]], axis=0)
            else:
                last_w[h] = got[:n]
        if s < 3:
            g = g + moved(g, lambda c: row_dim(c, 0, s))
        if s < 2:
            w_rows = jnp.concatenate(
                [w_rows, moved(w_rows, lambda c: y_dim(c, s))], axis=0
            )
    w_other = moved(w_rows, lambda c: "c")
    got = moved(g, lambda c: y_dim(c, 1))
    g = g + jnp.concatenate([got[64:], got[:64]], axis=0)
    g = jnp.concatenate([g, moved(g, lambda c: y_dim(c, 0))], axis=0)
    g_other = moved(g, lambda c: "c")

    part = update_first(tab, matrix, wc, w_rows, w_other, g, g_other, rh, rl, ch, cl)
    q_pieces = (q[0], last_q[0], q[1], last_q[1])
    return tuple(update_last(tab, part, last_w, basis_rows, q_pieces, rh, rl))


def solution(mesh):
    placed = (P("row", ("col", "grp")), P(("col", "grp"), "row"), P("row", None), P())
    return jax.shard_map(
        on_device,
        mesh=mesh,
        in_specs=placed,
        out_specs=(P("row", ("col", "grp")), P(("col", "grp"), "row")),
        check_vma=False,
    )
```
